32 devices in a mesh: fsdp: 8 (over z, y), rep: 4 (over x, core).
Axes of the slice: x: 2, y: 2, z: 4, core: 2. Of those that a mesh axis runs over, the one named last changes fastest.
Arguments:
- tokens: bfloat16 [32768, 768], P(('fsdp', 'rep')), may hold values from -6 to 6
- seg_ids: int32 [64, 512], P(('fsdp', 'rep')), may hold values from 0 to 3, never falling along the last dimension, each value on 1 to 256 neighbouring positions
- w_qkv: bfloat16 [768, 2304], P(('fsdp', 'rep')), may hold values from -0.21875 to 0.21875
- w_out: bfloat16 [768, 768], P(('fsdp', 'rep')), may hold values from -1.25 to 1.25
- w_up: bfloat16 [768, 3072], P(('fsdp', 'rep')), may hold values from -0.21875 to 0.21875
- w_down: bfloat16 [3072, 768], P(('fsdp', 'rep')), may hold values from -0.109375 to 0.109375
- ln_gain: bfloat16 [2, 768], P(None, ('fsdp', 'rep')), may hold values from 0.099609375 to 1.8984375
- ln_bias: bfloat16 [2, 768], P(None, ('fsdp', 'rep')), may hold values from -3 to 3
- bias_attn: bfloat16 [3, 768], P(None, ('fsdp', 'rep')), may hold values from -3 to 3
- bias_up: bfloat16 [3072], P(('fsdp', 'rep')), may hold values from -3 to 3
- bias_down: bfloat16 [768], P(('fsdp', 'rep')), may hold values from -3 to 3
- grad_out: bfloat16 [32768, 768], P(('fsdp', 'rep')), may hold values from -6 to 6
Outputs:
- layer_out: bfloat16 [32768, 768], P(('fsdp', 'rep'))
- grad_tokens: bfloat16 [32768, 768], P(('fsdp', 'rep'))
- grad_w_qkv: float32 [768, 2304], P(('fsdp', 'rep'))
- grad_w_out: float32 [768, 768], P(('fsdp', 'rep'))
- grad_w_up: float32 [768, 3072], P(('fsdp', 'rep'))
- grad_w_down: float32 [3072, 768], P(('fsdp', 'rep'))
- grad_ln_gain: float32 [2, 768], P(None, ('fsdp', 'rep'))
- grad_ln_bias: float32 [2, 768], P(None, ('fsdp', 'rep'))
- grad_bias_attn: float32 [3, 768], P(None, ('fsdp', 'rep'))
- grad_bias_up: float32 [3072], P(('fsdp', 'rep'))
- grad_bias_down: float32 [768], P(('fsdp', 'rep'))
The draws below stay inside these ranges and needn't reach their ends.
Inputs may be any that keep to these rules, and one draw needn't show every extreme that they name: `seg_ids`: within each row (one micro-batch of 512 tokens) sequence numbers never fall; each sequence has 1 to 256 tokens and one has exactly 256.
All inputs are finite; a program needn't handle non-finite values.
Results may differ from the reference program's by a relative error of at most 0.012.
Values may be sent and summed in bfloat16 or wider, within the bound.
A program may use at most 192 MiB of HBM per device.

```python
import math
import jax
import jax.numpy as jnp
import numpy as np
from jax import lax

D = 768
HEADS = 12
FF = 3072
HEAD = 64
MB_TOK = 512
SEGS = 4
SEG_MOST = 256
TOKENS = 32768
BATCHES = 64


def with_spikes(entries, rng, source, target, blocks, factor):
    def block_of(position):
        return (jnp.arange(entries.shape[position]) // (entries.shape[position] // blocks)).reshape((-1,) + (1,) * (entries.ndim - 1 - position))

    one_side = jax.random.permutation(rng, blocks)[block_of(target)]
    other_side = (block_of(target) + blocks // 2) % blocks
    return jnp.where((block_of(source) == one_side) | (block_of(source) == other_side), factor * entries, entries)


def block_levels(own_key, dims, split, smallest, high):
    factor_of, own = 1.0, jax.random.fold_in(own_key, 6)
    for axis_at, shards_of in split:
        steps = jnp.exp(jax.random.uniform(jax.random.fold_in(own, axis_at), (shards_of,), jnp.float32, smallest / len(split), high / len(split)))
        factor_of = factor_of * jnp.repeat(steps, dims[axis_at] // shards_of).reshape([-1 if axis == axis_at else 1 for axis in range(len(dims))])
    return factor_of


def profile(number_of, total, bound, skew):
    loads = [(1 << 20) // math.isqrt(rank ** skew) + 1 for rank in range(2, number_of + 1)]
    spare, counts = total - bound - (number_of - 1), [1] * (number_of - 1)
    while spare > 0:
        movable = [i for i in range(number_of - 1) if counts[i] < bound]
        whole, remaining = sum([loads[i] for i in movable]), spare
        for i in movable:
            more = min(bound - counts[i], max(1, remaining * loads[i] // whole), spare)
            counts[i] = counts[i] + more
            spare = spare - more
    return np.array([bound] + counts)


def uneven_parts(stream_key, number_of, total, most, slope):
    if number_of == 2:
        one = jax.random.randint(stream_key, (), max(1, total - most), min(most, total - 1) + 1)
        return jnp.stack([one, total - one])
    lengths = jnp.asarray(profile(number_of, total, most, slope), jnp.int32)
    pairs = (number_of - 1) // 2
    donor, receiver = lengths[1:1 + 2 * pairs:2], lengths[2:2 + 2 * pairs:2]
    margin = jnp.minimum(donor - 1, most - receiver)
    passed = jax.random.randint(jax.random.fold_in(stream_key, 1), (pairs,), 0, 1 << 20) % (margin + 1)
    lengths = lengths.at[1:1 + 2 * pairs:2].set(donor - passed).at[2:2 + 2 * pairs:2].set(receiver + passed)
    return lengths[jax.random.permutation(jax.random.fold_in(stream_key, 2), number_of)]


def normal_values(key, shape, scale, bound, cuts=(), kind=jnp.bfloat16):
    factor_of = block_levels(key, shape, cuts, -0.22, 0.18) if cuts else 1.0
    result = jax.random.normal(key, shape, jnp.float32) * scale * factor_of
    return jnp.minimum(jnp.maximum(result, -bound), bound).astype(kind)


def noise_with(own_key, shape, deviation, bound, cuts, heavy, dtype=jnp.bfloat16):
    array = deviation * jax.random.normal(own_key, shape, jnp.float32)
    if cuts:
        array = array * block_levels(own_key, shape, cuts, -0.22, 0.18)
    return jnp.clip(with_spikes(array, jax.random.fold_in(own_key, 3), *heavy), -bound, bound).astype(dtype)


def setup_inputs(seed: int = 0) -> dict:
    key_of = jax.random.split(jax.random.key(seed), 13)
    tokens = normal_values(key_of[0], (TOKENS, D), 1.0, 6.0, ((0, 32),))
    seg_ids = jax.vmap(lambda own: jnp.searchsorted(jnp.cumsum(uneven_parts(own, SEGS, MB_TOK, SEG_MOST, 2)), jnp.arange(MB_TOK), side="right"))(jax.random.split(key_of[1], BATCHES)).reshape((BATCHES, MB_TOK)).astype(jnp.int32)
    w_qkv = normal_values(key_of[2], (D, 3 * D), D ** -0.5, 0.21875, ((0, 32),))
    w_out = normal_values(key_of[3], (D, D), (D // 32) ** -0.5, 1.25, ((0, 32),))
    w_up = normal_values(key_of[4], (D, FF), D ** -0.5, 0.21875, ((0, 32),))
    w_down = normal_values(key_of[5], (FF, D), FF ** -0.5, 0.109375, ((0, 32),))
    ln_gain = jnp.clip(1.0 + 0.18 * jax.random.normal(key_of[6], (2, D), jnp.float32), 0.099609375, 1.8984375).astype(jnp.bfloat16)
    ln_bias = normal_values(key_of[7], (2, D), 0.5, 3.0, ((1, 32),))
    bias_attn = normal_values(key_of[8], (3, D), 0.5, 3.0, ((1, 32),))
    bias_up = normal_values(key_of[9], (FF,), 0.5, 3.0, ((0, 32),))
    bias_down = normal_values(key_of[10], (D,), 0.5, 3.0, ((0, 32),))
    grad_out = noise_with(key_of[11], (TOKENS, D), 1.0, 6.0, ((0, 32),), (0, 1, 32, 2.75))
    return {"tokens": tokens, "seg_ids": seg_ids, "w_qkv": w_qkv, "w_out": w_out, "w_up": w_up, "w_down": w_down, "ln_gain": ln_gain, "ln_bias": ln_bias, "bias_attn": bias_attn, "bias_up": bias_up, "bias_down": bias_down, "grad_out": grad_out}


EPSILON = 1e-05
SCORE_SCALE = 0.125
MASK_VALUE = -1000000000.0

@jax.custom_vjp
def low(v):
    return lax.optimization_barrier(v.astype(jnp.bfloat16)).astype(jnp.float32)

@jax.custom_vjp
def low_back(v):
    return v

def low_keep(v):
    return (low(v), None)

def low_pass(kept, grad):
    return (grad,)

def back_keep(v):
    return (v, None)

def back_low(kept, grad):
    return (low(grad),)
low.defvjp(low_keep, low_pass)
low_back.defvjp(back_keep, back_low)

def norm_rows(inputs, scaling, offset):
    row_mean = lax.optimization_barrier(jnp.mean(inputs, axis=-1, keepdims=True))
    centred = inputs - row_mean
    spread = lax.optimization_barrier(jnp.mean(centred * centred, axis=-1, keepdims=True))
    return centred * lax.rsqrt(spread + EPSILON) * scaling + offset

def matmul(left, right):
    return jnp.dot(left, right, precision=lax.Precision.HIGHEST, preferred_element_type=jnp.float32)

def layer_block(weights, token_rows, segment_row):
    w_qkv, w_out, w_up, w_down, ln_gain, ln_bias, bias_attn, bias_up, bias_down = weights
    row_count = token_rows.shape[0]
    normed = low(norm_rows(token_rows, ln_gain[0], ln_bias[0]))
    zero_bias = jnp.zeros((D,), jnp.float32)
    joined = matmul(normed, w_qkv) + jnp.concatenate([bias_attn[0], zero_bias, bias_attn[1]])
    joined = low(low_back(joined))
    queries = joined[:, :D].reshape(row_count, HEADS, HEAD)
    key_rows = joined[:, D:2 * D].reshape(row_count, HEADS, HEAD)
    values = joined[:, 2 * D:].reshape(row_count, HEADS, HEAD)
    scores = jnp.einsum('qhd,khd->hqk', queries, key_rows, precision=lax.Precision.HIGHEST) * SCORE_SCALE
    scores = low_back(scores)
    places = jnp.arange(row_count)
    allowed = (segment_row[:, None] == segment_row[None, :]) & (places[None, :] <= places[:, None])
    scores = jnp.where(allowed[None], scores, MASK_VALUE)
    attn_probs = low(jax.nn.softmax(scores, axis=-1))
    attended = jnp.einsum('hqk,khd->qhd', attn_probs, values, precision=lax.Precision.HIGHEST)
    attended = low(low_back(attended.reshape(row_count, D)))
    residual = token_rows + low_back(matmul(attended, w_out) + bias_attn[2])
    second = low(norm_rows(residual, ln_gain[1], ln_bias[1]))
    pre_act = low_back(matmul(second, w_up) + bias_up)
    active = low(jax.nn.gelu(pre_act))
    return residual + low_back(matmul(active, w_down) + bias_down)

def forward_all(weights, tokens_all, segment_ids):
    blocks = tokens_all.reshape(segment_ids.shape[0], segment_ids.shape[1], D)
    checked = jax.checkpoint(layer_block)

    def one_block(block_pair):
        return checked(weights, block_pair[0], block_pair[1])
    outputs = lax.map(one_block, (blocks, segment_ids))
    return outputs.reshape(tokens_all.shape[0], D)

def reference(tokens, seg_ids, w_qkv, w_out, w_up, w_down, ln_gain, ln_bias, bias_attn, bias_up, bias_down, grad_out):
    weights = tuple((tensor.astype(jnp.float32) for tensor in (w_qkv, w_out, w_up, w_down, ln_gain, ln_bias, bias_attn, bias_up, bias_down)))

    def forward_fixed(weight_set, token_set):
        return forward_all(weight_set, token_set, seg_ids)
    layer_out, pullback = jax.vjp(forward_fixed, weights, tokens.astype(jnp.float32))
    grad_weights, grad_tokens = pullback(grad_out.astype(jnp.float32))
    return (layer_out.astype(jnp.bfloat16), grad_tokens.astype(jnp.bfloat16), grad_weights[0], grad_weights[1], grad_weights[2], grad_weights[3], grad_weights[4], grad_weights[5], grad_weights[6], grad_weights[7], grad_weights[8])
```

```python
import functools
import jax
import jax.numpy as jnp
from jax import lax
from jax.experimental import pallas as pl
from jax.experimental.pallas import tpu as pltpu
from jax.sharding import PartitionSpec as P

HEAD = 64
PAIR = 128
REACH = 256
EPSILON = 1e-05
SCORE_SCALE = 0.125
MASK_VALUE = -1000000000.0
AXES = ("fsdp", "rep")
MESH = pl.DeviceIdType.MESH
MIB = 1 << 20


def bits_of(sizes):
    out = []
    for axis, size in zip(AXES, sizes):
        weight = size // 2
        while weight:
            out.append((axis, weight))
            weight //= 2
    return out


def powers(sizes):
    return all(size & (size - 1) == 0 for size in sizes)


def orders_of(count):
    near = count - 1
    rest = list(range(near))
    if count == 5:
        base = [[0, 1, 2, 3], [3, 0, 1, 2], [2, 3, 0, 1]]
    else:
        third = max(1, len(rest) // 3)
        base = [rest[k * third :] + rest[: k * third] for k in range(3)]
    return [order + [near] for order in base]


def position(bits):
    place = {axis: lax.axis_index(axis) for axis in AXES}
    mine = [lax.rem(place[axis] // weight, 2) for axis, weight in bits]
    partners = []
    for (axis, weight), own in zip(bits, mine):
        there = dict(place)
        there[axis] = place[axis] + weight * (1 - 2 * own)
        partners.append(tuple(there[a] for a in AXES))
    return mine, partners


def greet(partners):
    barrier = pltpu.get_barrier_semaphore()
    for partner in partners:
        pl.semaphore_signal(barrier, inc=1, device_id=partner, device_id_type=MESH)
    pl.semaphore_wait(barrier, len(partners))


def parts_of(widths):
    pieces = []
    for tensor, width in enumerate(widths):
        if width % (3 * 128):
            pieces.append((tensor, 0, 0, width))
        else:
            third = width // 3
            pieces += [(tensor, k, k * third, third) for k in range(3)]
    return pieces


def gather_kernel(bits, pieces, count, *refs):
    shards, wholes = refs[:count], refs[count : 2 * count]
    send_sems, recv_sems, own_sems = refs[2 * count :]
    depth = len(bits)
    orders = orders_of(depth)
    mine, partners = position(bits)
    own = [
        pltpu.make_async_copy(shards[t], wholes[t].at[tuple(mine)], own_sems.at[t])
        for t in range(count)
    ]
    for copy in own:
        copy.start()
    greet(partners)
    for copy in own:
        copy.wait()

    def step(number, stage):
        tensor, order, first, columns = pieces[number]
        sequence = orders[order]
        done = sequence[:stage]
        where = tuple(slice(None) if k in done else mine[k] for k in range(depth))
        block = wholes[tensor].at[where + (slice(None), pl.ds(first, columns))]
        return pltpu.make_async_remote_copy(
            src_ref=block,
            dst_ref=block,
            send_sem=send_sems.at[number, stage],
            recv_sem=recv_sems.at[number, stage],
            device_id=partners[sequence[stage]],
            device_id_type=MESH,
        )

    for number in range(len(pieces)):
        step(number, 0).start()
    for stage in range(1, depth):
        for number in range(len(pieces)):
            step(number, stage - 1).wait_recv()
            step(number, stage).start()
    for number in range(len(pieces)):
        step(number, depth - 1).wait_recv()
    for stage in range(depth):
        for number in range(len(pieces)):
            step(number, stage).wait_send()


def gather_all(shards, sizes, collective_id):
    bits = bits_of(sizes)
    depth = len(bits)
    pieces = parts_of([shard.shape[1] for shard in shards])
    count = len(shards)
    total = sum(shard.size * shard.dtype.itemsize for shard in shards)
    wholes = pl.pallas_call(
        functools.partial(gather_kernel, bits, pieces, count),
        out_shape=[jax.ShapeDtypeStruct((2,) * depth + s.shape, s.dtype) for s in shards],
        in_specs=[pl.BlockSpec(memory_space=pl.ANY)] * count,
        out_specs=[pl.BlockSpec(memory_space=pl.ANY)] * count,
        scratch_shapes=[
            pltpu.SemaphoreType.DMA((len(pieces), depth)),
            pltpu.SemaphoreType.DMA((len(pieces), depth)),
            pltpu.SemaphoreType.DMA((count,)),
        ],
        compiler_params=pltpu.CompilerParams(collective_id=collective_id, has_side_effects=True),
        cost_estimate=pl.CostEstimate(
            flops=0, bytes_accessed=total << (depth + 1), transcendentals=0
        ),
    )(*shards)
    return [w.reshape((-1,) + w.shape[depth + 1 :]) for w in wholes]


def scatter_kernel(bits, pieces, count, *refs):
    parts, sums = refs[:count], refs[count : 2 * count]
    depth = len(bits)
    number_of = len(pieces)
    lands = refs[2 * count : 2 * count + number_of * depth]
    send_sems, recv_sems = refs[2 * count + number_of * depth :]
    orders = [list(reversed(order)) for order in orders_of(depth)]
    mine, partners = position(bits)
    greet(partners)

    def left_after(order, stage):
        gone = orders[order][:stage]
        return [k for k in range(depth) if k not in gone]

    def half(number, stage, whose, rest):
        tensor, order, first, columns = pieces[number]
        bit = orders[order][stage]
        side = mine[bit] if whose else 1 - mine[bit]
        index, rest = [], list(rest)
        for k in left_after(order, stage):
            index.append(side if k == bit else rest.pop(0))
        if stage == 0:
            return parts[tensor], tuple(index) + (slice(None), pl.ds(first, columns))
        return lands[number * depth + stage - 1], tuple(index)

    def step(number, stage):
        tensor, order, first, columns = pieces[number]
        buffer, index = half(number, stage, False, [slice(None)] * (depth - 1 - stage))
        return pltpu.make_async_remote_copy(
            src_ref=buffer.at[index],
            dst_ref=lands[number * depth + stage],
            send_sem=send_sems.at[number, stage],
            recv_sem=recv_sems.at[number, stage],
            device_id=partners[orders[order][stage]],
            device_id_type=MESH,
        )

    def settle(number, stage):
        tensor, order, first, columns = pieces[number]
        land = lands[number * depth + stage]
        free = depth - 1 - stage

        def one(i, carry):
            rest = [lax.rem(i // (1 << (free - 1 - k)), 2) for k in range(free)]
            buffer, index = half(number, stage, True, rest)
            value = buffer[index].astype(jnp.float32) + land[tuple(rest)].astype(jnp.float32)
            land[tuple(rest)] = value.astype(land.dtype)
            return carry

        if free:
            lax.fori_loop(0, 1 << free, one, 0)
        else:
            buffer, index = half(number, stage, True, [])
            value = buffer[index].astype(jnp.float32) + land[...].astype(jnp.float32)
            sums[tensor][:, pl.ds(first, columns)] = value

    for number in range(number_of):
        step(number, 0).start()
    for stage in range(depth):
        for number in range(number_of):
            step(number, stage).wait_recv()
            settle(number, stage)
            if stage + 1 < depth:
                step(number, stage + 1).start()
    for stage in range(depth):
        for number in range(number_of):
            step(number, stage).wait_send()


def scatter_all(totals, sizes, collective_id):
    bits = bits_of(sizes)
    depth = len(bits)
    devices = 1 << depth
    count = len(totals)
    parts = [
        t.reshape((2,) * depth + (t.shape[0] // devices, t.shape[1])) for t in totals
    ]
    pieces = parts_of([t.shape[1] for t in totals])
    lands = []
    for tensor, order, first, columns in pieces:
        rows = parts[tensor].shape[depth]
        for stage in range(depth):
            lands.append(
                pltpu.VMEM((2,) * (depth - 1 - stage) + (rows, columns), parts[tensor].dtype)
            )
    moved = sum(t.size * t.dtype.itemsize for t in totals)
    return pl.pallas_call(
        functools.partial(scatter_kernel, bits, pieces, count),
        out_shape=[
            jax.ShapeDtypeStruct((t.shape[0] // devices, t.shape[1]), jnp.float32) for t in totals
        ],
        in_specs=[pl.BlockSpec(memory_space=pltpu.VMEM)] * count,
        out_specs=[pl.BlockSpec(memory_space=pltpu.VMEM)] * count,
        scratch_shapes=lands
        + [
            pltpu.SemaphoreType.DMA((len(pieces), depth)),
            pltpu.SemaphoreType.DMA((len(pieces), depth)),
        ],
        compiler_params=pltpu.CompilerParams(
            collective_id=collective_id, has_side_effects=True, vmem_limit_bytes=56 * MIB
        ),
        cost_estimate=pl.CostEstimate(flops=0, bytes_accessed=2 * moved, transcendentals=0),
    )(*parts)


def dot_nt(left, right):
    return lax.dot_general(
        left, right, (((1,), (1,)), ((), ())), preferred_element_type=jnp.float32
    )


def dot_tn(left, right):
    return lax.dot_general(
        left, right, (((0,), (0,)), ((), ())), preferred_element_type=jnp.float32
    )


def windows(length):
    step = PAIR if length % PAIR == 0 else length
    for row in range(0, length, step):
        yield row, step, max(0, row - (REACH if step == PAIR else length)), row + step


def masks_of(seg_row_ref, seg_col_ref, row, step, low, high):
    places = row + lax.broadcasted_iota(jnp.int32, (step, high - low), 0)
    others = low + lax.broadcasted_iota(jnp.int32, (step, high - low), 1)
    same = seg_col_ref[0, row : row + step, :] == seg_row_ref[0, :, low:high]
    return same & (others <= places)


def first_half(shape):
    return lax.broadcasted_iota(jnp.int32, shape, 1) < HEAD


def attention_kernel(joined_ref, seg_row_ref, seg_col_ref, att_ref, norm_ref):
    length = joined_ref.shape[0]
    width = att_ref.shape[1]
    for row, step, low, high in windows(length):
        allowed = masks_of(seg_row_ref, seg_col_ref, row, step, low, high)

        def pair(number, carry):
            at = pl.multiple_of(number * PAIR, PAIR)
            queries = joined_ref[row : row + step, pl.ds(at, PAIR)] * SCORE_SCALE
            keys = joined_ref[low:high, pl.ds(width + at, PAIR)]
            values = joined_ref[low:high, pl.ds(2 * width + at, PAIR)]
            left = first_half((step, PAIR))
            outs, norms = [], []
            for lanes in (left, ~left):
                scores = dot_nt(jnp.where(lanes, queries, 0).astype(jnp.bfloat16), keys)
                scores = jnp.where(allowed, scores, MASK_VALUE)
                top = jnp.max(scores, axis=-1, keepdims=True)
                weights = jnp.exp(scores - top)
                total = jnp.sum(weights, axis=-1, keepdims=True)
                probs = (weights * (1.0 / total)).astype(jnp.bfloat16)
                outs.append(jnp.dot(probs, values, preferred_element_type=jnp.float32))
                norms.append(jnp.broadcast_to(top + jnp.log(total), (step, PAIR)))
            att_ref[row : row + step, pl.ds(at, PAIR)] = jnp.where(left, *outs).astype(
                jnp.bfloat16
            )
            norm_ref[row : row + step, pl.ds(at, PAIR)] = jnp.where(left, *norms)
            return carry

        lax.fori_loop(0, width // PAIR, pair, 0)


def attention_back_kernel(
    joined_ref, grad_ref, norm_ref, seg_row_ref, seg_col_ref, out_ref, keys_sum, values_sum
):
    length, width = grad_ref.shape
    keys_sum[...] = jnp.zeros_like(keys_sum)
    values_sum[...] = jnp.zeros_like(values_sum)
    for row, step, low, high in windows(length):
        allowed = masks_of(seg_row_ref, seg_col_ref, row, step, low, high)

        def pair(number, carry):
            at = pl.multiple_of(number * PAIR, PAIR)
            queries = joined_ref[row : row + step, pl.ds(at, PAIR)]
            keys = joined_ref[low:high, pl.ds(width + at, PAIR)]
            values = joined_ref[low:high, pl.ds(2 * width + at, PAIR)]
            grads = grad_ref[row : row + step, pl.ds(at, PAIR)]
            norms = norm_ref[row : row + step, pl.ds(at, PAIR)]
            scaled = queries * SCORE_SCALE
            left = first_half((step, PAIR))
            tall = first_half((high - low, PAIR))
            d_query, d_keys, d_values = [], [], []
            for lanes, lane in ((left, 0), (~left, HEAD)):
                scores = dot_nt(jnp.where(lanes, scaled, 0).astype(jnp.bfloat16), keys)
                probs = jnp.where(allowed, jnp.exp(scores - norms[:, lane : lane + 1]), 0.0)
                d_probs = dot_nt(jnp.where(lanes, grads, 0).astype(jnp.bfloat16), values)
                inner = jnp.sum(probs * d_probs, axis=-1, keepdims=True)
                d_scores = (probs * (d_probs - inner)).astype(jnp.bfloat16)
                d_query.append(jnp.dot(d_scores, keys, preferred_element_type=jnp.float32))
                d_keys.append(dot_tn(d_scores, queries))
                d_values.append(dot_tn(probs.astype(jnp.bfloat16), grads))
            out_ref[row : row + step, pl.ds(at, PAIR)] = (
                jnp.where(left, *d_query) * SCORE_SCALE
            ).astype(jnp.bfloat16)
            keys_sum[low:high, pl.ds(at, PAIR)] += jnp.where(tall, *d_keys)
            values_sum[low:high, pl.ds(at, PAIR)] += jnp.where(tall, *d_values)
            return carry

        lax.fori_loop(0, width // PAIR, pair, 0)
    out_ref[:, width : 2 * width] = (keys_sum[...] * SCORE_SCALE).astype(jnp.bfloat16)
    out_ref[:, 2 * width :] = values_sum[...].astype(jnp.bfloat16)


def seg_views(seg_ids):
    batches, length = seg_ids.shape
    return seg_ids.reshape(batches, 1, length), seg_ids.reshape(batches, length, 1)


def row_spec(length, width):
    return pl.BlockSpec((length, width), lambda b: (b, 0))


def seg_specs(length):
    return [
        pl.BlockSpec((1, 1, length), lambda b: (b, 0, 0)),
        pl.BlockSpec((1, length, 1), lambda b: (b, 0, 0)),
    ]


def attention(joined, seg_ids):
    batches, length = seg_ids.shape
    rows = joined.shape[0]
    width = joined.shape[1] // 3
    return pl.pallas_call(
        attention_kernel,
        grid=(batches,),
        in_specs=[row_spec(length, 3 * width)] + seg_specs(length),
        out_specs=[row_spec(length, width), row_spec(length, width)],
        out_shape=[
            jax.ShapeDtypeStruct((rows, width), jnp.bfloat16),
            jax.ShapeDtypeStruct((rows, width), jnp.float32),
        ],
        compiler_params=pltpu.CompilerParams(vmem_limit_bytes=40 * MIB),
    )(joined, *seg_views(seg_ids))


def attention_back(joined, grad_att, norms, seg_ids):
    batches, length = seg_ids.shape
    rows, width = grad_att.shape
    return pl.pallas_call(
        attention_back_kernel,
        grid=(batches,),
        in_specs=[row_spec(length, 3 * width), row_spec(length, width), row_spec(length, width)]
        + seg_specs(length),
        out_specs=row_spec(length, 3 * width),
        out_shape=jax.ShapeDtypeStruct((rows, 3 * width), jnp.bfloat16),
        scratch_shapes=[
            pltpu.VMEM((length, width), jnp.float32),
            pltpu.VMEM((length, width), jnp.float32),
        ],
        compiler_params=pltpu.CompilerParams(vmem_limit_bytes=40 * MIB),
    )(joined, grad_att, norms, *seg_views(seg_ids))


def norm_rows(inputs, scaling, offset):
    row_mean = jnp.mean(inputs, axis=-1, keepdims=True)
    centred = inputs - row_mean
    spread = jnp.mean(centred * centred, axis=-1, keepdims=True)
    return centred * lax.rsqrt(spread + EPSILON) * scaling + offset


def pack_small(gain, shift, attn, up, down):
    width = -(-max(gain.shape[1], up.shape[0] + down.shape[0]) // 128) * 128
    rows = jnp.concatenate([gain, shift, attn], axis=0).astype(jnp.float32)
    last = jnp.concatenate([up, down]).astype(jnp.float32)
    return jnp.concatenate(
        [
            jnp.pad(rows, ((0, 0), (0, width - rows.shape[1]))),
            jnp.pad(last, (0, width - last.shape[0]))[None],
        ],
        axis=0,
    )


def fetch(w_qkv, w_out, w_up, w_down, small, sizes):
    devices = sizes[0] * sizes[1]
    if powers(sizes) and w_qkv.shape[0] % 8 == 0:
        wholes = gather_all([w_qkv, w_out, w_up, w_down, small], sizes, 1)
    else:
        wholes = [
            lax.all_gather(w, AXES, axis=0, tiled=True)
            for w in (w_qkv, w_out, w_up, w_down, small)
        ]
    return wholes[:4], wholes[4].reshape(devices, small.shape[0], small.shape[1])


def settle_all(totals, small, sizes):
    flat = small.reshape(-1, small.shape[2])
    devices = sizes[0] * sizes[1]
    if powers(sizes) and (totals[0].shape[0] // devices) % 8 == 0:
        sums = scatter_all(list(totals) + [flat], sizes, 2)
    else:
        sums = [
            lax.psum_scatter(
                t.astype(jnp.float32), AXES, scatter_dimension=0, tiled=True
            )
            for t in list(totals) + [flat]
        ]
    return sums[:4], sums[4]


def local(
    sizes,
    tokens,
    seg_ids,
    w_qkv,
    w_out,
    w_up,
    w_down,
    ln_gain,
    ln_bias,
    bias_attn,
    bias_up,
    bias_down,
    grad_out,
):
    devices = sizes[0] * sizes[1]
    model_width = tokens.shape[1]
    own = ln_gain.shape[1]
    own_up = bias_up.shape[0]
    (w_qkv, w_out, w_up, w_down), small = fetch(
        w_qkv,
        w_out,
        w_up,
        w_down,
        pack_small(ln_gain, ln_bias, bias_attn, bias_up, bias_down),
        sizes,
    )
    features = jnp.swapaxes(small[:, :7, :own], 0, 1).reshape(7, devices * own)
    gains, shifts, attn_bias = features[0:2], features[2:4], features[4:7]
    up_bias = small[:, 7, :own_up].reshape(-1)
    down_bias = small[:, 7, own_up : own_up + own].reshape(-1)

    rows_float = tokens.astype(jnp.float32)
    normed, norm_one = jax.vjp(norm_rows, rows_float, gains[0], shifts[0])
    normed_low = normed.astype(jnp.bfloat16)
    zero_bias = jnp.zeros((model_width,), jnp.float32)
    qkv_bias = jnp.concatenate([attn_bias[0], zero_bias, attn_bias[1]])
    joined = (jnp.dot(normed_low, w_qkv, preferred_element_type=jnp.float32) + qkv_bias).astype(
        jnp.bfloat16
    )
    attended, norms = attention(joined, seg_ids)
    residual = (
        rows_float + jnp.dot(attended, w_out, preferred_element_type=jnp.float32) + attn_bias[2]
    )
    second, norm_two = jax.vjp(norm_rows, residual, gains[1], shifts[1])
    second_low = second.astype(jnp.bfloat16)
    pre_act = jnp.dot(second_low, w_up, preferred_element_type=jnp.float32) + up_bias
    active, gelu_back = jax.vjp(jax.nn.gelu, pre_act)
    active_low = active.astype(jnp.bfloat16)
    layer_out = (
        residual + jnp.dot(active_low, w_down, preferred_element_type=jnp.float32) + down_bias
    ).astype(jnp.bfloat16)

    grad_float = grad_out.astype(jnp.float32)
    down_sum = dot_tn(active_low, grad_out).astype(jnp.bfloat16)
    downb_sum = jnp.sum(grad_float, axis=0)
    grad_active = dot_nt(grad_out, w_down)
    grad_pre = gelu_back(grad_active)[0].astype(jnp.bfloat16)
    up_sum = dot_tn(second_low, grad_pre).astype(jnp.bfloat16)
    upb_sum = jnp.sum(grad_pre.astype(jnp.float32), axis=0)
    grad_second = dot_nt(grad_pre, w_up)
    grad_resid, gain_two, shift_two = norm_two(grad_second)
    grad_resid = grad_resid + grad_float
    grad_resid_low = grad_resid.astype(jnp.bfloat16)
    out_sum = dot_tn(attended, grad_resid_low).astype(jnp.bfloat16)
    bias_out_grad = jnp.sum(grad_resid_low.astype(jnp.float32), axis=0)
    grad_att = dot_nt(grad_resid_low, w_out).astype(jnp.bfloat16)
    grad_joined = attention_back(joined, grad_att, norms, seg_ids)
    qkv_sum = dot_tn(normed_low, grad_joined).astype(jnp.bfloat16)
    joined_bias = jnp.sum(grad_joined.astype(jnp.float32), axis=0)
    grad_normed = dot_nt(grad_joined, w_qkv)
    grad_input, gain_one, shift_one = norm_one(grad_normed)
    grad_tokens = (grad_resid + grad_input).astype(jnp.bfloat16)

    features = jnp.stack(
        [
            gain_one,
            gain_two,
            shift_one,
            shift_two,
            joined_bias[:model_width],
            joined_bias[2 * model_width :],
            bias_out_grad,
        ]
    )
    features = jnp.swapaxes(features.reshape(7, devices, own), 0, 1)
    last = jnp.concatenate(
        [upb_sum.reshape(devices, own_up), downb_sum.reshape(devices, own)], axis=1
    )
    width = small.shape[2]
    packed = jnp.concatenate(
        [
            jnp.pad(features, ((0, 0), (0, 0), (0, width - own))),
            jnp.pad(last, ((0, 0), (0, width - last.shape[1])))[:, None],
        ],
        axis=1,
    )
    sums, packed = settle_all([qkv_sum, out_sum, up_sum, down_sum], packed, sizes)
    return (
        layer_out,
        grad_tokens,
        *sums,
        packed[0:2, :own],
        packed[2:4, :own],
        packed[4:7, :own],
        packed[7, :own_up],
        packed[7, own_up : own_up + own],
    )


def solution(mesh):
    return jax.shard_map(
        functools.partial(local, (mesh.shape["fsdp"], mesh.shape["rep"])),
        mesh=mesh,
        in_specs=(
            P(("fsdp", "rep"), None),
            P(("fsdp", "rep"), None),
            P(("fsdp", "rep"), None),
            P(("fsdp", "rep"), None),
            P(("fsdp", "rep"), None),
            P(("fsdp", "rep"), None),
            P(None, ("fsdp", "rep")),
            P(None, ("fsdp", "rep")),
            P(None, ("fsdp", "rep")),
            P(("fsdp", "rep")),
            P(("fsdp", "rep")),
            P(("fsdp", "rep"), None),
        ),
        out_specs=(
            P(("fsdp", "rep"), None),
            P(("fsdp", "rep"), None),
            P(("fsdp", "rep"), None),
            P(("fsdp", "rep"), None),
            P(("fsdp", "rep"), None),
            P(("fsdp", "rep"), None),
            P(None, ("fsdp", "rep")),
            P(None, ("fsdp", "rep")),
            P(None, ("fsdp", "rep")),
            P(("fsdp", "rep")),
            P(("fsdp", "rep")),
        ),
        check_vma=False,
    )
```

```python
import functools
import jax
import jax.numpy as jnp
from jax import lax
from jax.experimental import pallas as pl
from jax.experimental.pallas import tpu as pltpu
from jax.sharding import PartitionSpec as P

HEAD = 64
PAIR = 128
REACH = 256
EPSILON = 1e-05
SCORE_SCALE = 0.125
MASK_VALUE = -1000000000.0
AXES = ("fsdp", "rep")
MESH = pl.DeviceIdType.MESH
MIB = 1 << 20
GELU_IN = 0.7978845608028654
GELU_CUBE = 0.044715


def bits_of(sizes):
    out = []
    for axis, size in zip(AXES, sizes):
        weight = size // 2
        while weight:
            out.append((axis, weight))
            weight //= 2
    return out


def powers(sizes):
    return all(size & (size - 1) == 0 for size in sizes)


def orders_of(count):
    near = count - 1
    rest = list(range(near))
    if count == 5:
        base = [[0, 1, 2, 3], [3, 0, 1, 2], [2, 3, 0, 1]]
    else:
        third = max(1, len(rest) // 3)
        base = [rest[k * third :] + rest[: k * third] for k in range(3)]
    return [order + [near] for order in base]


def position(bits):
    place = {axis: lax.axis_index(axis) for axis in AXES}
    mine = [lax.rem(place[axis] // weight, 2) for axis, weight in bits]
    partners = []
    for (axis, weight), own in zip(bits, mine):
        there = dict(place)
        there[axis] = place[axis] + weight * (1 - 2 * own)
        partners.append(tuple(there[a] for a in AXES))
    return mine, partners


def greet(partners):
    barrier = pltpu.get_barrier_semaphore()
    for partner in partners:
        pl.semaphore_signal(barrier, inc=1, device_id=partner, device_id_type=MESH)
    pl.semaphore_wait(barrier, len(partners))


def parts_of(widths):
    pieces = []
    for tensor, width in enumerate(widths):
        if width % (3 * 128):
            pieces.append((tensor, 0, 0, width))
        else:
            third = width // 3
            pieces += [(tensor, k, k * third, third) for k in range(3)]
    return pieces


def gather_kernel(bits, pieces, count, *refs):
    run_gather(bits, pieces, refs[:count], refs[count : 2 * count], refs[2 * count :])


def run_gather(bits, pieces, shards, wholes, sems, work=lambda stage: None):
    count = len(shards)
    send_sems, recv_sems, own_sems = sems
    depth = len(bits)
    orders = orders_of(depth)
    mine, partners = position(bits)
    own = [
        pltpu.make_async_copy(shards[t], wholes[t].at[tuple(mine)], own_sems.at[t])
        for t in range(count)
    ]
    for copy in own:
        copy.start()
    greet(partners)
    for copy in own:
        copy.wait()

    def step(number, stage):
        tensor, order, first, columns = pieces[number]
        sequence = orders[order]
        done = sequence[:stage]
        where = tuple(slice(None) if k in done else mine[k] for k in range(depth))
        block = wholes[tensor].at[where + (slice(None), pl.ds(first, columns))]
        return pltpu.make_async_remote_copy(
            src_ref=block,
            dst_ref=block,
            send_sem=send_sems.at[number, stage],
            recv_sem=recv_sems.at[number, stage],
            device_id=partners[sequence[stage]],
            device_id_type=MESH,
        )

    for number in range(len(pieces)):
        step(number, 0).start()
    work(0)
    for stage in range(1, depth):
        for number in range(len(pieces)):
            step(number, stage - 1).wait_recv()
            step(number, stage).start()
        work(stage)
    for number in range(len(pieces)):
        step(number, depth - 1).wait_recv()
    for stage in range(depth):
        for number in range(len(pieces)):
            step(number, stage).wait_send()


def gather_sems(pieces, depth, count):
    return [
        pltpu.SemaphoreType.DMA((len(pieces), depth)),
        pltpu.SemaphoreType.DMA((len(pieces), depth)),
        pltpu.SemaphoreType.DMA((count,)),
    ]


def gather_all(shards, sizes, collective_id):
    bits = bits_of(sizes)
    depth = len(bits)
    pieces = parts_of([shard.shape[1] for shard in shards])
    count = len(shards)
    total = sum(shard.size * shard.dtype.itemsize for shard in shards)
    wholes = pl.pallas_call(
        functools.partial(gather_kernel, bits, pieces, count),
        out_shape=[jax.ShapeDtypeStruct((2,) * depth + s.shape, s.dtype) for s in shards],
        in_specs=[pl.BlockSpec(memory_space=pl.ANY)] * count,
        out_specs=[pl.BlockSpec(memory_space=pl.ANY)] * count,
        scratch_shapes=gather_sems(pieces, depth, count),
        compiler_params=pltpu.CompilerParams(collective_id=collective_id, has_side_effects=True),
        cost_estimate=pl.CostEstimate(
            flops=0, bytes_accessed=total << (depth + 1), transcendentals=0
        ),
    )(*shards)
    return [w.reshape((-1,) + w.shape[depth + 1 :]) for w in wholes]


def scatter_kernel(bits, pieces, count, *refs):
    run_scatter(bits, pieces, refs[:count], refs[count : 2 * count], refs[2 * count :])


def run_scatter(bits, pieces, parts, sums, scratch, work=lambda stage: None):
    depth = len(bits)
    number_of = len(pieces)
    lands = scratch[: number_of * depth]
    send_sems, recv_sems = scratch[number_of * depth :]
    orders = [list(reversed(order)) for order in orders_of(depth)]
    mine, partners = position(bits)
    greet(partners)

    def left_after(order, stage):
        gone = orders[order][:stage]
        return [k for k in range(depth) if k not in gone]

    def half(number, stage, whose, rest):
        tensor, order, first, columns = pieces[number]
        bit = orders[order][stage]
        side = mine[bit] if whose else 1 - mine[bit]
        index, rest = [], list(rest)
        for k in left_after(order, stage):
            index.append(side if k == bit else rest.pop(0))
        if stage == 0:
            return parts[tensor], tuple(index) + (slice(None), pl.ds(first, columns))
        return lands[number * depth + stage - 1], tuple(index)

    def step(number, stage):
        tensor, order, first, columns = pieces[number]
        buffer, index = half(number, stage, False, [slice(None)] * (depth - 1 - stage))
        return pltpu.make_async_remote_copy(
            src_ref=buffer.at[index],
            dst_ref=lands[number * depth + stage],
            send_sem=send_sems.at[number, stage],
            recv_sem=recv_sems.at[number, stage],
            device_id=partners[orders[order][stage]],
            device_id_type=MESH,
        )

    def settle(number, stage):
        tensor, order, first, columns = pieces[number]
        land = lands[number * depth + stage]
        free = depth - 1 - stage

        def one(i, carry):
            rest = [lax.rem(i // (1 << (free - 1 - k)), 2) for k in range(free)]
            buffer, index = half(number, stage, True, rest)
            value = buffer[index].astype(jnp.float32) + land[tuple(rest)].astype(jnp.float32)
            land[tuple(rest)] = value.astype(land.dtype)
            return carry

        if free:
            lax.fori_loop(0, 1 << free, one, 0)
        else:
            buffer, index = half(number, stage, True, [])
            value = buffer[index].astype(jnp.float32) + land[...].astype(jnp.float32)
            sums[tensor][:, pl.ds(first, columns)] = value

    for number in range(number_of):
        step(number, 0).start()
    for stage in range(depth):
        work(stage)
        for number in range(number_of):
            step(number, stage).wait_recv()
            settle(number, stage)
            if stage + 1 < depth:
                step(number, stage + 1).start()
    for stage in range(depth):
        for number in range(number_of):
            step(number, stage).wait_send()


def scatter_parts(totals, depth):
    parts = [
        t.reshape((2,) * depth + (t.shape[0] // (1 << depth), t.shape[1])) for t in totals
    ]
    pieces = parts_of([t.shape[1] for t in totals])
    lands = []
    for tensor, order, first, columns in pieces:
        rows = parts[tensor].shape[depth]
        for stage in range(depth):
            lands.append(
                pltpu.VMEM((2,) * (depth - 1 - stage) + (rows, columns), parts[tensor].dtype)
            )
    sems = [pltpu.SemaphoreType.DMA((len(pieces), depth))] * 2
    return parts, pieces, lands + sems


def scatter_all(totals, sizes, collective_id):
    bits = bits_of(sizes)
    depth = len(bits)
    devices = 1 << depth
    count = len(totals)
    parts, pieces, scratch = scatter_parts(totals, depth)
    moved = sum(t.size * t.dtype.itemsize for t in totals)
    return pl.pallas_call(
        functools.partial(scatter_kernel, bits, pieces, count),
        out_shape=[
            jax.ShapeDtypeStruct((t.shape[0] // devices, t.shape[1]), jnp.float32) for t in totals
        ],
        in_specs=[pl.BlockSpec(memory_space=pltpu.VMEM)] * count,
        out_specs=[pl.BlockSpec(memory_space=pltpu.VMEM)] * count,
        scratch_shapes=scratch,
        compiler_params=pltpu.CompilerParams(
            collective_id=collective_id, has_side_effects=True, vmem_limit_bytes=56 * MIB
        ),
        cost_estimate=pl.CostEstimate(flops=0, bytes_accessed=2 * moved, transcendentals=0),
    )(*parts)


def dot_nt(left, right):
    return lax.dot_general(
        left, right, (((1,), (1,)), ((), ())), preferred_element_type=jnp.float32
    )


def dot_tn(left, right):
    return lax.dot_general(
        left, right, (((0,), (0,)), ((), ())), preferred_element_type=jnp.float32
    )


def windows(length):
    step = PAIR if length % PAIR == 0 else length
    for row in range(0, length, step):
        yield row, step, max(0, row - (REACH if step == PAIR else length)), row + step


def masks_of(seg_row_ref, seg_col_ref, batch, length, row, step, low, high):
    places = row + lax.broadcasted_iota(jnp.int32, (step, high - low), 0)
    others = low + lax.broadcasted_iota(jnp.int32, (step, high - low), 1)
    begin = batch * length + row
    same = seg_col_ref[begin : begin + step, :] == seg_row_ref[batch : batch + 1, low:high]
    return same & (others <= places)


def first_half(shape):
    return lax.broadcasted_iota(jnp.int32, shape, 1) < HEAD


def attend_rows(width, joined_ref, seg_row_ref, seg_col_ref, att_ref, norm_ref, batch, window):
    length = seg_row_ref.shape[1]
    row, step, low, high = window
    base = batch * length
    allowed = masks_of(seg_row_ref, seg_col_ref, batch, length, row, step, low, high)
    mine, seen = pl.ds(base + row, step), pl.ds(base + low, high - low)

    def pair(number, carry):
        at = pl.multiple_of(number * PAIR, PAIR)
        queries = joined_ref[mine, pl.ds(at, PAIR)] * SCORE_SCALE
        keys = joined_ref[seen, pl.ds(width + at, PAIR)]
        values = joined_ref[seen, pl.ds(2 * width + at, PAIR)]
        left = first_half((step, PAIR))
        outs, norms = [], []
        for lanes in (left, ~left):
            scores = dot_nt(jnp.where(lanes, queries, 0).astype(jnp.bfloat16), keys)
            scores = jnp.where(allowed, scores, MASK_VALUE)
            top = jnp.max(scores, axis=-1, keepdims=True)
            weights = jnp.exp(scores - top)
            total = jnp.sum(weights, axis=-1, keepdims=True)
            probs = (weights * (1.0 / total)).astype(jnp.bfloat16)
            outs.append(jnp.dot(probs, values, preferred_element_type=jnp.float32))
            norms.append(jnp.broadcast_to(top + jnp.log(total), (step, PAIR)))
        att_ref[mine, pl.ds(at, PAIR)] = jnp.where(left, *outs).astype(jnp.bfloat16)
        norm_ref[mine, pl.ds(at, PAIR)] = jnp.where(left, *norms)
        return carry

    lax.fori_loop(0, width // PAIR, pair, 0, unroll=2)


def attend_rows_back(
    width,
    joined_ref,
    grad_ref,
    norm_ref,
    seg_row_ref,
    seg_col_ref,
    out_ref,
    keys_sum,
    values_sum,
    batch,
    window,
):
    length = seg_row_ref.shape[1]
    row, step, low, high = window
    base = batch * length
    allowed = masks_of(seg_row_ref, seg_col_ref, batch, length, row, step, low, high)
    mine, seen = pl.ds(base + row, step), pl.ds(base + low, high - low)

    def pair(number, carry):
        at = pl.multiple_of(number * PAIR, PAIR)
        queries = joined_ref[mine, pl.ds(at, PAIR)]
        keys = joined_ref[seen, pl.ds(width + at, PAIR)]
        values = joined_ref[seen, pl.ds(2 * width + at, PAIR)]
        grads = grad_ref[mine, pl.ds(at, PAIR)]
        norms = norm_ref[mine, pl.ds(at, PAIR)]
        scaled = queries * SCORE_SCALE
        left = first_half((step, PAIR))
        tall = first_half((high - low, PAIR))
        d_query, d_keys, d_values = [], [], []
        for lanes, lane in ((left, 0), (~left, HEAD)):
            scores = dot_nt(jnp.where(lanes, scaled, 0).astype(jnp.bfloat16), keys)
            scores = jnp.where(allowed, scores, MASK_VALUE)
            probs = jnp.exp(scores - norms[:, lane : lane + 1])
            d_probs = dot_nt(jnp.where(lanes, grads, 0).astype(jnp.bfloat16), values)
            inner = jnp.sum(probs * d_probs, axis=-1, keepdims=True)
            d_scores = (probs * (d_probs - inner)).astype(jnp.bfloat16)
            d_query.append(jnp.dot(d_scores, keys, preferred_element_type=jnp.float32))
            d_keys.append(dot_tn(d_scores, queries))
            d_values.append(dot_tn(probs.astype(jnp.bfloat16), grads))
        out_ref[mine, pl.ds(at, PAIR)] = (jnp.where(left, *d_query) * SCORE_SCALE).astype(
            jnp.bfloat16
        )
        keys_sum[seen, pl.ds(at, PAIR)] += jnp.where(tall, *d_keys)
        values_sum[seen, pl.ds(at, PAIR)] += jnp.where(tall, *d_values)
        return carry

    lax.fori_loop(0, width // PAIR, pair, 0, unroll=2)


def shared_out(batches, length, shares):
    units = [(b, w) for w in windows(length) for b in range(batches)]
    cost = sum(w[3] - w[2] for b, w in units)
    stages, spent, limit, at = [[] for _ in shares], 0, shares[0], 0
    for b, w in units:
        while spent * sum(shares) >= limit * cost and at + 1 < len(shares):
            at += 1
            limit += shares[at]
        stages[at].append((b, w))
        spent += w[3] - w[2]
    return stages


def attention_kernel(bits, pieces, count, *refs):
    joined_ref, seg_row_ref, seg_col_ref = refs[:3]
    shards = refs[3 : 3 + count]
    att_ref, norm_ref = refs[3 + count : 5 + count]
    wholes, sems = refs[5 + count : 5 + 2 * count], refs[5 + 2 * count :]
    batches, length = seg_row_ref.shape
    shares = (1, 2, 3, 6, 6) if len(bits) == 5 else (1,) * max(1, len(bits))
    stages = shared_out(batches, length, shares)

    def work(stage):
        for batch, window in stages[stage]:
            attend_rows(
                att_ref.shape[1],
                joined_ref,
                seg_row_ref,
                seg_col_ref,
                att_ref,
                norm_ref,
                batch,
                window,
            )

    if count:
        run_gather(bits, pieces, shards, wholes, sems, work)
    else:
        for stage in range(len(shares)):
            work(stage)


def attention(joined, seg_ids, shards, sizes, collective_id):
    batches, length = seg_ids.shape
    rows = joined.shape[0]
    width = joined.shape[1] // 3
    count = len(shards)
    bits = bits_of(sizes)
    depth = len(bits)
    pieces = parts_of([shard.shape[1] for shard in shards])
    remote = dict(collective_id=collective_id, has_side_effects=True) if count else {}
    near, far = pl.BlockSpec(memory_space=pltpu.VMEM), pl.BlockSpec(memory_space=pl.ANY)
    att, norms, *wholes = pl.pallas_call(
        functools.partial(attention_kernel, bits, pieces, count),
        in_specs=[near] * 3 + [far] * count,
        out_specs=[near] * 2 + [far] * count,
        out_shape=[
            jax.ShapeDtypeStruct((rows, width), jnp.bfloat16),
            jax.ShapeDtypeStruct((rows, width), jnp.float32),
        ]
        + [jax.ShapeDtypeStruct((2,) * depth + s.shape, s.dtype) for s in shards],
        scratch_shapes=gather_sems(pieces, depth, count) if count else [],
        compiler_params=pltpu.CompilerParams(vmem_limit_bytes=40 * MIB, **remote),
        cost_estimate=pl.CostEstimate(
            flops=100 * rows * width * length, bytes_accessed=rows * width * 12, transcendentals=0
        ),
    )(joined, seg_ids, seg_ids.reshape(rows, 1), *shards)
    return att, norms, [w.reshape((-1,) + w.shape[depth + 1 :]) for w in wholes]


def attention_back_kernel(bits, pieces, count, *refs):
    joined_ref, grad_ref, norm_ref, seg_row_ref, seg_col_ref = refs[:5]
    parts = refs[5 : 5 + count]
    out_ref = refs[5 + count]
    sums = refs[6 + count : 6 + 2 * count]
    keys_sum, values_sum = refs[6 + 2 * count : 8 + 2 * count]
    scratch = refs[8 + 2 * count :]
    batches, length = seg_row_ref.shape
    width = grad_ref.shape[1]
    shares = (4, 6, 4, 2, 2) if len(bits) == 5 else (1,) * max(1, len(bits))
    stages = shared_out(batches, length, shares)

    def work(stage):
        if stage == 0:
            keys_sum[...] = jnp.zeros_like(keys_sum)
            values_sum[...] = jnp.zeros_like(values_sum)
        for batch, window in stages[stage]:
            attend_rows_back(
                width,
                joined_ref,
                grad_ref,
                norm_ref,
                seg_row_ref,
                seg_col_ref,
                out_ref,
                keys_sum,
                values_sum,
                batch,
                window,
            )
        if stage == len(shares) - 1:
            out_ref[:, width : 2 * width] = (keys_sum[...] * SCORE_SCALE).astype(jnp.bfloat16)
            out_ref[:, 2 * width :] = values_sum[...].astype(jnp.bfloat16)

    if count:
        run_scatter(bits, pieces, parts, sums, scratch, work)
    else:
        for stage in range(len(shares)):
            work(stage)


def attention_back(joined, grad_att, norms, seg_ids, totals, sizes, collective_id):
    batches, length = seg_ids.shape
    rows, width = grad_att.shape
    count = len(totals)
    bits = bits_of(sizes)
    depth = len(bits)
    parts, pieces, scratch = scatter_parts(totals, depth) if count else ([], [], [])
    remote = dict(collective_id=collective_id, has_side_effects=True) if count else {}
    near = pl.BlockSpec(memory_space=pltpu.VMEM)
    out, *sums = pl.pallas_call(
        functools.partial(attention_back_kernel, bits, pieces, count),
        in_specs=[near] * (5 + count),
        out_specs=[near] * (1 + count),
        out_shape=[jax.ShapeDtypeStruct((rows, 3 * width), jnp.bfloat16)]
        + [
            jax.ShapeDtypeStruct((t.shape[0] >> depth, t.shape[1]), jnp.float32) for t in totals
        ],
        scratch_shapes=[pltpu.VMEM((rows, width), jnp.float32)] * 2 + scratch,
        compiler_params=pltpu.CompilerParams(vmem_limit_bytes=56 * MIB, **remote),
        cost_estimate=pl.CostEstimate(
            flops=100 * rows * width * length, bytes_accessed=rows * width * 12, transcendentals=0
        ),
    )(joined, grad_att, norms, seg_ids, seg_ids.reshape(rows, 1), *parts)
    return out, sums


def ffn_kernel(
    second_ref, grad_ref, up_ref, down_ref, bias_ref, out_ref, back_ref, up_sum, down_sum, bias_sum
):
    @pl.when(pl.program_id(0) == 0)
    def _():
        out_ref[...] = jnp.zeros_like(out_ref)
        back_ref[...] = jnp.zeros_like(back_ref)

    second, grad = second_ref[...], grad_ref[...]
    pre = jnp.dot(second, up_ref[...], preferred_element_type=jnp.float32) + bias_ref[...]
    square = pre * pre
    bend = jnp.tanh(GELU_IN * pre * (1.0 + GELU_CUBE * square))
    half = 0.5 + 0.5 * bend
    active = (pre * half).astype(jnp.bfloat16)
    slope = half + 0.5 * pre * (1.0 - bend * bend) * (
        GELU_IN * (1.0 + 3.0 * GELU_CUBE * square)
    )
    out_ref[...] += jnp.dot(active, down_ref[...], preferred_element_type=jnp.float32)
    grad_pre = dot_nt(grad, down_ref[...]) * slope
    low = grad_pre.astype(jnp.bfloat16)
    down_sum[...] = dot_tn(active, grad).astype(down_sum.dtype)
    up_sum[...] = dot_tn(second, low).astype(up_sum.dtype)
    bias_sum[...] = jnp.sum(low.astype(jnp.float32), axis=0, keepdims=True)
    back_ref[...] += dot_nt(low, up_ref[...])


def feed_forward(second, grad_out, w_up, w_down, up_bias):
    rows, width = second.shape
    hidden = w_up.shape[1]
    block = 512 if hidden % 512 == 0 else hidden
    fixed = pl.BlockSpec((rows, width), lambda j: (0, 0))
    across = pl.BlockSpec((width, block), lambda j: (0, j))
    along = pl.BlockSpec((block, width), lambda j: (j, 0))
    line = pl.BlockSpec((1, block), lambda j: (0, j))
    return pl.pallas_call(
        ffn_kernel,
        grid=(hidden // block,),
        in_specs=[fixed, fixed, across, along, line],
        out_specs=[fixed, fixed, across, along, line],
        out_shape=[
            jax.ShapeDtypeStruct((rows, width), jnp.float32),
            jax.ShapeDtypeStruct((rows, width), jnp.float32),
            jax.ShapeDtypeStruct((width, hidden), jnp.bfloat16),
            jax.ShapeDtypeStruct((hidden, width), jnp.bfloat16),
            jax.ShapeDtypeStruct((1, hidden), jnp.float32),
        ],
        compiler_params=pltpu.CompilerParams(vmem_limit_bytes=56 * MIB),
        cost_estimate=pl.CostEstimate(
            flops=12 * rows * width * hidden,
            bytes_accessed=8 * width * hidden + 16 * rows * width,
            transcendentals=rows * hidden,
        ),
    )(second, grad_out, w_up, w_down, up_bias[None])


def norm_rows(inputs, scaling, offset):
    row_mean = jnp.mean(inputs, axis=-1, keepdims=True)
    centred = inputs - row_mean
    spread = jnp.mean(centred * centred, axis=-1, keepdims=True)
    return centred * lax.rsqrt(spread + EPSILON) * scaling + offset


def pack_small(gain, shift, attn, up, down):
    width = -(-max(gain.shape[1], up.shape[0] + down.shape[0]) // 128) * 128
    rows = jnp.concatenate([gain, shift, attn], axis=0).astype(jnp.float32)
    last = jnp.concatenate([up, down]).astype(jnp.float32)
    return jnp.concatenate(
        [
            jnp.pad(rows, ((0, 0), (0, width - rows.shape[1]))),
            jnp.pad(last, (0, width - last.shape[0]))[None],
        ],
        axis=0,
    )


def own_exchange(sizes, shard_rows):
    return powers(sizes) and shard_rows % 8 == 0


def gathered(shard):
    return lax.all_gather(shard, AXES, axis=0, tiled=True)


def scattered(total):
    return lax.psum_scatter(total, AXES, scatter_dimension=0, tiled=True)


def local(
    sizes,
    tokens,
    seg_ids,
    w_qkv,
    w_out,
    w_up,
    w_down,
    ln_gain,
    ln_bias,
    bias_attn,
    bias_up,
    bias_down,
    grad_out,
):
    devices = sizes[0] * sizes[1]
    model_width = tokens.shape[1]
    own = ln_gain.shape[1]
    own_up = bias_up.shape[0]
    direct = own_exchange(sizes, w_qkv.shape[0])
    small = pack_small(ln_gain, ln_bias, bias_attn, bias_up, bias_down)
    small_shape = small.shape
    w_down = gathered(w_down)
    if direct:
        w_qkv, small = gather_all([w_qkv, small], sizes, 1)
    else:
        w_qkv, small, w_out, w_up = (gathered(t) for t in (w_qkv, small, w_out, w_up))
    small = small.reshape((devices,) + small_shape)
    features = jnp.swapaxes(small[:, :7, :own], 0, 1).reshape(7, devices * own)
    gains, shifts, attn_bias = features[0:2], features[2:4], features[4:7]
    up_bias = small[:, 7, :own_up].reshape(-1)
    down_bias = small[:, 7, own_up : own_up + own].reshape(-1)

    rows_float = tokens.astype(jnp.float32)
    normed, norm_one = jax.vjp(norm_rows, rows_float, gains[0], shifts[0])
    normed_low = normed.astype(jnp.bfloat16)
    zero_bias = jnp.zeros((model_width,), jnp.float32)
    qkv_bias = jnp.concatenate([attn_bias[0], zero_bias, attn_bias[1]])
    joined = (jnp.dot(normed_low, w_qkv, preferred_element_type=jnp.float32) + qkv_bias).astype(
        jnp.bfloat16
    )
    attended, norms, moved = attention(
        joined, seg_ids, [w_out, w_up] if direct else [], sizes, 2
    )
    if direct:
        w_out, w_up = moved
    residual = (
        rows_float + jnp.dot(attended, w_out, preferred_element_type=jnp.float32) + attn_bias[2]
    )
    second, norm_two = jax.vjp(norm_rows, residual, gains[1], shifts[1])
    second_low = second.astype(jnp.bfloat16)
    ffn_out, grad_second, up_sum, down_sum, upb_sum = feed_forward(
        second_low, grad_out, w_up, w_down, up_bias
    )
    layer_out = (residual + ffn_out + down_bias).astype(jnp.bfloat16)
    down_sum = scattered(down_sum).astype(jnp.float32)

    grad_float = grad_out.astype(jnp.float32)
    downb_sum = jnp.sum(grad_float, axis=0)
    grad_resid, gain_two, shift_two = norm_two(grad_second)
    grad_resid = grad_resid + grad_float
    grad_resid_low = grad_resid.astype(jnp.bfloat16)
    out_sum = dot_tn(attended, grad_resid_low).astype(jnp.bfloat16)
    bias_out_grad = jnp.sum(grad_resid_low.astype(jnp.float32), axis=0)
    grad_att = dot_nt(grad_resid_low, w_out).astype(jnp.bfloat16)
    grad_joined, moved = attention_back(
        joined, grad_att, norms, seg_ids, [up_sum, out_sum] if direct else [], sizes, 3
    )
    if direct:
        up_sum, out_sum = moved
    qkv_sum = dot_tn(normed_low, grad_joined).astype(jnp.bfloat16)
    joined_bias = jnp.sum(grad_joined.astype(jnp.float32), axis=0)
    grad_normed = dot_nt(grad_joined, w_qkv)
    grad_input, gain_one, shift_one = norm_one(grad_normed)
    grad_tokens = (grad_resid + grad_input).astype(jnp.bfloat16)

    features = jnp.stack(
        [
            gain_one,
            gain_two,
            shift_one,
            shift_two,
            joined_bias[:model_width],
            joined_bias[2 * model_width :],
            bias_out_grad,
        ]
    )
    features = jnp.swapaxes(features.reshape(7, devices, own), 0, 1)
    last = jnp.concatenate(
        [upb_sum.reshape(devices, own_up), downb_sum.reshape(devices, own)], axis=1
    )
    width = small.shape[2]
    packed = jnp.concatenate(
        [
            jnp.pad(features, ((0, 0), (0, 0), (0, width - own))),
            jnp.pad(last, ((0, 0), (0, width - last.shape[1])))[:, None],
        ],
        axis=1,
    )
    packed = packed.reshape(-1, width)
    if direct:
        qkv_sum, packed = scatter_all([qkv_sum, packed], sizes, 4)
    else:
        qkv_sum, out_sum, up_sum, packed = (
            scattered(t.astype(jnp.float32)) for t in (qkv_sum, out_sum, up_sum, packed)
        )
    return (
        layer_out,
        grad_tokens,
        qkv_sum,
        out_sum,
        up_sum,
        down_sum,
        packed[0:2, :own],
        packed[2:4, :own],
        packed[4:7, :own],
        packed[7, :own_up],
        packed[7, own_up : own_up + own],
    )


def solution(mesh):
    return jax.shard_map(
        functools.partial(local, (mesh.shape["fsdp"], mesh.shape["rep"])),
        mesh=mesh,
        in_specs=(
            P(("fsdp", "rep"), None),
            P(("fsdp", "rep"), None),
            P(("fsdp", "rep"), None),
            P(("fsdp", "rep"), None),
            P(("fsdp", "rep"), None),
            P(("fsdp", "rep"), None),
            P(None, ("fsdp", "rep")),
            P(None, ("fsdp", "rep")),
            P(None, ("fsdp", "rep")),
            P(("fsdp", "rep")),
            P(("fsdp", "rep")),
            P(("fsdp", "rep"), None),
        ),
        out_specs=(
            P(("fsdp", "rep"), None),
            P(("fsdp", "rep"), None),
            P(("fsdp", "rep"), None),
            P(("fsdp", "rep"), None),
            P(("fsdp", "rep"), None),
            P(("fsdp", "rep"), None),
            P(None, ("fsdp", "rep")),
            P(None, ("fsdp", "rep")),
            P(None, ("fsdp", "rep")),
            P(("fsdp", "rep")),
            P(("fsdp", "rep")),
        ),
        check_vma=False,
    )
```

```python
import functools
import jax
import jax.numpy as jnp
from jax import lax
from jax.experimental import pallas as pl
from jax.experimental.pallas import tpu as pltpu
from jax.sharding import PartitionSpec as P

HEAD = 64
PAIR = 128
REACH = 256
EPSILON = 1e-05
SCORE_SCALE = 0.125
MASK_VALUE = -1000000000.0
AXES = ("fsdp", "rep")
MESH = pl.DeviceIdType.MESH
MIB = 1 << 20
GELU_IN = 0.7978845608028654
GELU_CUBE = 0.044715


def bits_of(sizes):
    out = []
    for axis, size in zip(AXES, sizes):
        weight = size // 2
        while weight:
            out.append((axis, weight))
            weight //= 2
    return out


def powers(sizes):
    return all(size & (size - 1) == 0 for size in sizes)


def orders_of(count):
    near = count - 1
    rest = list(range(near))
    if count == 5:
        base = [[0, 1, 2, 3], [3, 0, 1, 2], [2, 3, 0, 1]]
    else:
        third = max(1, len(rest) // 3)
        base = [rest[k * third :] + rest[: k * third] for k in range(3)]
    return [order + [near] for order in base]


def position(bits):
    place = {axis: lax.axis_index(axis) for axis in AXES}
    mine = [lax.rem(place[axis] // weight, 2) for axis, weight in bits]
    partners = []
    for (axis, weight), own in zip(bits, mine):
        there = dict(place)
        there[axis] = place[axis] + weight * (1 - 2 * own)
        partners.append(tuple(there[a] for a in AXES))
    return mine, partners


def greet(partners):
    barrier = pltpu.get_barrier_semaphore()
    for partner in partners:
        pl.semaphore_signal(barrier, inc=1, device_id=partner, device_id_type=MESH)
    pl.semaphore_wait(barrier, len(partners))


def parts_of(widths):
    pieces = []
    for tensor, width in enumerate(widths):
        if width % (3 * 128):
            pieces.append((tensor, 0, 0, width))
        else:
            third = width // 3
            pieces += [(tensor, k, k * third, third) for k in range(3)]
    return pieces


def gather_kernel(bits, pieces, count, *refs):
    run_gather(bits, pieces, refs[:count], refs[count : 2 * count], refs[2 * count :])


def run_gather(bits, pieces, shards, wholes, sems, work=lambda stage: None):
    count = len(shards)
    send_sems, recv_sems, own_sems = sems
    depth = len(bits)
    orders = orders_of(depth)
    mine, partners = position(bits)
    own = [
        pltpu.make_async_copy(shards[t], wholes[t].at[tuple(mine)], own_sems.at[t])
        for t in range(count)
    ]
    for copy in own:
        copy.start()
    greet(partners)
    for copy in own:
        copy.wait()

    def step(number, stage):
        tensor, order, first, columns = pieces[number]
        sequence = orders[order]
        done = sequence[:stage]
        where = tuple(slice(None) if k in done else mine[k] for k in range(depth))
        block = wholes[tensor].at[where + (slice(None), pl.ds(first, columns))]
        return pltpu.make_async_remote_copy(
            src_ref=block,
            dst_ref=block,
            send_sem=send_sems.at[number, stage],
            recv_sem=recv_sems.at[number, stage],
            device_id=partners[sequence[stage]],
            device_id_type=MESH,
        )

    for number in range(len(pieces)):
        step(number, 0).start()
    work(0)
    for stage in range(1, depth):
        for number in range(len(pieces)):
            step(number, stage - 1).wait_recv()
            step(number, stage).start()
        work(stage)
    for number in range(len(pieces)):
        step(number, depth - 1).wait_recv()
    for stage in range(depth):
        for number in range(len(pieces)):
            step(number, stage).wait_send()


def gather_sems(pieces, depth, count):
    return [
        pltpu.SemaphoreType.DMA((len(pieces), depth)),
        pltpu.SemaphoreType.DMA((len(pieces), depth)),
        pltpu.SemaphoreType.DMA((count,)),
    ]


def gather_all(shards, sizes, collective_id):
    bits = bits_of(sizes)
    depth = len(bits)
    pieces = parts_of([shard.shape[1] for shard in shards])
    count = len(shards)
    total = sum(shard.size * shard.dtype.itemsize for shard in shards)
    wholes = pl.pallas_call(
        functools.partial(gather_kernel, bits, pieces, count),
        out_shape=[jax.ShapeDtypeStruct((2,) * depth + s.shape, s.dtype) for s in shards],
        in_specs=[pl.BlockSpec(memory_space=pl.ANY)] * count,
        out_specs=[pl.BlockSpec(memory_space=pl.ANY)] * count,
        scratch_shapes=gather_sems(pieces, depth, count),
        compiler_params=pltpu.CompilerParams(collective_id=collective_id, has_side_effects=True),
        cost_estimate=pl.CostEstimate(
            flops=0, bytes_accessed=total << (depth + 1), transcendentals=0
        ),
    )(*shards)
    return [w.reshape((-1,) + w.shape[depth + 1 :]) for w in wholes]


def scatter_kernel(bits, pieces, count, *refs):
    run_scatter(bits, pieces, refs[:count], refs[count : 2 * count], refs[2 * count :])


def run_scatter(bits, pieces, parts, sums, scratch, work=lambda stage: None):
    depth = len(bits)
    number_of = len(pieces)
    lands = scratch[: number_of * depth]
    send_sems, recv_sems = scratch[number_of * depth :]
    orders = [list(reversed(order)) for order in orders_of(depth)]
    mine, partners = position(bits)
    greet(partners)

    def left_after(order, stage):
        gone = orders[order][:stage]
        return [k for k in range(depth) if k not in gone]

    def half(number, stage, whose, rest):
        tensor, order, first, columns = pieces[number]
        bit = orders[order][stage]
        side = mine[bit] if whose else 1 - mine[bit]
        index, rest = [], list(rest)
        for k in left_after(order, stage):
            index.append(side if k == bit else rest.pop(0))
        if stage == 0:
            return parts[tensor], tuple(index) + (slice(None), pl.ds(first, columns))
        return lands[number * depth + stage - 1], tuple(index)

    def step(number, stage):
        tensor, order, first, columns = pieces[number]
        buffer, index = half(number, stage, False, [slice(None)] * (depth - 1 - stage))
        return pltpu.make_async_remote_copy(
            src_ref=buffer.at[index],
            dst_ref=lands[number * depth + stage],
            send_sem=send_sems.at[number, stage],
            recv_sem=recv_sems.at[number, stage],
            device_id=partners[orders[order][stage]],
            device_id_type=MESH,
        )

    def settle(number, stage):
        tensor, order, first, columns = pieces[number]
        land = lands[number * depth + stage]
        free = depth - 1 - stage

        def one(i, carry):
            rest = [lax.rem(i // (1 << (free - 1 - k)), 2) for k in range(free)]
            buffer, index = half(number, stage, True, rest)
            value = buffer[index].astype(jnp.float32) + land[tuple(rest)].astype(jnp.float32)
            land[tuple(rest)] = value.astype(land.dtype)
            return carry

        if free:
            lax.fori_loop(0, 1 << free, one, 0)
        else:
            buffer, index = half(number, stage, True, [])
            value = buffer[index].astype(jnp.float32) + land[...].astype(jnp.float32)
            sums[tensor][:, pl.ds(first, columns)] = value

    for number in range(number_of):
        step(number, 0).start()
    for stage in range(depth):
        work(stage)
        for number in range(number_of):
            step(number, stage).wait_recv()
            settle(number, stage)
            if stage + 1 < depth:
                step(number, stage + 1).start()
    for stage in range(depth):
        for number in range(number_of):
            step(number, stage).wait_send()


def scatter_parts(totals, depth):
    parts = [
        t.reshape((2,) * depth + (t.shape[0] // (1 << depth), t.shape[1])) for t in totals
    ]
    pieces = parts_of([t.shape[1] for t in totals])
    lands = []
    for tensor, order, first, columns in pieces:
        rows = parts[tensor].shape[depth]
        for stage in range(depth):
            lands.append(
                pltpu.VMEM((2,) * (depth - 1 - stage) + (rows, columns), parts[tensor].dtype)
            )
    sems = [pltpu.SemaphoreType.DMA((len(pieces), depth))] * 2
    return parts, pieces, lands + sems


def scatter_all(totals, sizes, collective_id):
    bits = bits_of(sizes)
    depth = len(bits)
    devices = 1 << depth
    count = len(totals)
    parts, pieces, scratch = scatter_parts(totals, depth)
    moved = sum(t.size * t.dtype.itemsize for t in totals)
    return pl.pallas_call(
        functools.partial(scatter_kernel, bits, pieces, count),
        out_shape=[
            jax.ShapeDtypeStruct((t.shape[0] // devices, t.shape[1]), jnp.float32) for t in totals
        ],
        in_specs=[pl.BlockSpec(memory_space=pltpu.VMEM)] * count,
        out_specs=[pl.BlockSpec(memory_space=pltpu.VMEM)] * count,
        scratch_shapes=scratch,
        compiler_params=pltpu.CompilerParams(
            collective_id=collective_id, has_side_effects=True, vmem_limit_bytes=56 * MIB
        ),
        cost_estimate=pl.CostEstimate(flops=0, bytes_accessed=2 * moved, transcendentals=0),
    )(*parts)


def dot_nt(left, right):
    return lax.dot_general(
        left, right, (((1,), (1,)), ((), ())), preferred_element_type=jnp.float32
    )


def dot_tn(left, right):
    return lax.dot_general(
        left, right, (((0,), (0,)), ((), ())), preferred_element_type=jnp.float32
    )


def windows(length):
    step = PAIR if length % PAIR == 0 else length
    for row in range(0, length, step):
        yield row, step, max(0, row - (REACH if step == PAIR else length)), row + step


def masks_of(seg_row_ref, seg_col_ref, batch, length, row, step, low, high):
    places = row + lax.broadcasted_iota(jnp.int32, (step, high - low), 0)
    others = low + lax.broadcasted_iota(jnp.int32, (step, high - low), 1)
    begin = batch * length + row
    same = seg_col_ref[begin : begin + step, :] == seg_row_ref[batch : batch + 1, low:high]
    return same & (others <= places)


def first_half(shape):
    return lax.broadcasted_iota(jnp.int32, shape, 1) < HEAD


def attend_rows(width, joined_ref, seg_row_ref, seg_col_ref, att_ref, norm_ref, batch, window):
    length = seg_row_ref.shape[1]
    row, step, low, high = window
    base = batch * length
    allowed = masks_of(seg_row_ref, seg_col_ref, batch, length, row, step, low, high)
    mine, seen = pl.ds(base + row, step), pl.ds(base + low, high - low)

    def pair(number, carry):
        at = pl.multiple_of(number * PAIR, PAIR)
        queries = joined_ref[mine, pl.ds(at, PAIR)] * SCORE_SCALE
        keys = joined_ref[seen, pl.ds(width + at, PAIR)]
        values = joined_ref[seen, pl.ds(2 * width + at, PAIR)]
        left = first_half((step, PAIR))
        outs, norms = [], []
        for lanes in (left, ~left):
            scores = dot_nt(jnp.where(lanes, queries, 0).astype(jnp.bfloat16), keys)
            scores = jnp.where(allowed, scores, MASK_VALUE)
            top = jnp.max(scores, axis=-1, keepdims=True)
            weights = jnp.exp(scores - top)
            total = jnp.sum(weights, axis=-1, keepdims=True)
            probs = (weights * (1.0 / total)).astype(jnp.bfloat16)
            outs.append(jnp.dot(probs, values, preferred_element_type=jnp.float32))
            norms.append(jnp.broadcast_to(top + jnp.log(total), (step, PAIR)))
        att_ref[mine, pl.ds(at, PAIR)] = jnp.where(left, *outs).astype(jnp.bfloat16)
        norm_ref[mine, pl.ds(at, PAIR)] = jnp.where(left, *norms)
        return carry

    lax.fori_loop(0, width // PAIR, pair, 0, unroll=2)


def attend_rows_back(
    width,
    joined_ref,
    grad_ref,
    norm_ref,
    seg_row_ref,
    seg_col_ref,
    out_ref,
    keys_sum,
    values_sum,
    batch,
    window,
):
    length = seg_row_ref.shape[1]
    row, step, low, high = window
    base = batch * length
    allowed = masks_of(seg_row_ref, seg_col_ref, batch, length, row, step, low, high)
    mine, seen = pl.ds(base + row, step), pl.ds(base + low, high - low)

    def pair(number, carry):
        at = pl.multiple_of(number * PAIR, PAIR)
        queries = joined_ref[mine, pl.ds(at, PAIR)]
        keys = joined_ref[seen, pl.ds(width + at, PAIR)]
        values = joined_ref[seen, pl.ds(2 * width + at, PAIR)]
        grads = grad_ref[mine, pl.ds(at, PAIR)]
        norms = norm_ref[mine, pl.ds(at, PAIR)]
        scaled = queries * SCORE_SCALE
        left = first_half((step, PAIR))
        tall = first_half((high - low, PAIR))
        d_query, d_keys, d_values = [], [], []
        for lanes, lane in ((left, 0), (~left, HEAD)):
            scores = dot_nt(jnp.where(lanes, scaled, 0).astype(jnp.bfloat16), keys)
            scores = jnp.where(allowed, scores, MASK_VALUE)
            probs = jnp.exp(scores - norms[:, lane : lane + 1])
            d_probs = dot_nt(jnp.where(lanes, grads, 0).astype(jnp.bfloat16), values)
            inner = jnp.sum(probs * d_probs, axis=-1, keepdims=True)
            d_scores = (probs * (d_probs - inner)).astype(jnp.bfloat16)
            d_query.append(jnp.dot(d_scores, keys, preferred_element_type=jnp.float32))
            d_keys.append(dot_tn(d_scores, queries))
            d_values.append(dot_tn(probs.astype(jnp.bfloat16), grads))
        out_ref[mine, pl.ds(at, PAIR)] = (jnp.where(left, *d_query) * SCORE_SCALE).astype(
            jnp.bfloat16
        )
        keys_sum[seen, pl.ds(at, PAIR)] += jnp.where(tall, *d_keys)
        values_sum[seen, pl.ds(at, PAIR)] += jnp.where(tall, *d_values)
        return carry

    lax.fori_loop(0, width // PAIR, pair, 0, unroll=2)


def shared_out(batches, length, shares):
    units = [(b, w) for w in windows(length) for b in range(batches)]
    cost = sum(w[3] - w[2] for b, w in units)
    stages, spent, limit, at = [[] for _ in shares], 0, shares[0], 0
    for b, w in units:
        while spent * sum(shares) >= limit * cost and at + 1 < len(shares):
            at += 1
            limit += shares[at]
        stages[at].append((b, w))
        spent += w[3] - w[2]
    return stages


def attention_kernel(bits, pieces, count, *refs):
    joined_ref, seg_row_ref, seg_col_ref = refs[:3]
    shards = refs[3 : 3 + count]
    att_ref, norm_ref = refs[3 + count : 5 + count]
    wholes, sems = refs[5 + count : 5 + 2 * count], refs[5 + 2 * count :]
    batches, length = seg_row_ref.shape
    shares = (1, 2, 3, 6, 6) if len(bits) == 5 else (1,) * max(1, len(bits))
    stages = shared_out(batches, length, shares)

    def work(stage):
        for batch, window in stages[stage]:
            attend_rows(
                att_ref.shape[1],
                joined_ref,
                seg_row_ref,
                seg_col_ref,
                att_ref,
                norm_ref,
                batch,
                window,
            )

    if count:
        run_gather(bits, pieces, shards, wholes, sems, work)
    else:
        for stage in range(len(shares)):
            work(stage)


def attention(joined, seg_ids, shards, sizes, collective_id):
    batches, length = seg_ids.shape
    rows = joined.shape[0]
    width = joined.shape[1] // 3
    count = len(shards)
    bits = bits_of(sizes)
    depth = len(bits)
    pieces = parts_of([shard.shape[1] for shard in shards])
    remote = dict(collective_id=collective_id, has_side_effects=True) if count else {}
    near, far = pl.BlockSpec(memory_space=pltpu.VMEM), pl.BlockSpec(memory_space=pl.ANY)
    att, norms, *wholes = pl.pallas_call(
        functools.partial(attention_kernel, bits, pieces, count),
        in_specs=[near] * 3 + [far] * count,
        out_specs=[near] * 2 + [far] * count,
        out_shape=[
            jax.ShapeDtypeStruct((rows, width), jnp.bfloat16),
            jax.ShapeDtypeStruct((rows, width), jnp.float32),
        ]
        + [jax.ShapeDtypeStruct((2,) * depth + s.shape, s.dtype) for s in shards],
        scratch_shapes=gather_sems(pieces, depth, count) if count else [],
        compiler_params=pltpu.CompilerParams(vmem_limit_bytes=40 * MIB, **remote),
        cost_estimate=pl.CostEstimate(
            flops=100 * rows * width * length, bytes_accessed=rows * width * 12, transcendentals=0
        ),
    )(joined, seg_ids, seg_ids.reshape(rows, 1), *shards)
    return att, norms, [w.reshape((-1,) + w.shape[depth + 1 :]) for w in wholes]


def attention_back_kernel(bits, pieces, count, *refs):
    joined_ref, grad_ref, norm_ref, seg_row_ref, seg_col_ref = refs[:5]
    parts = refs[5 : 5 + count]
    out_ref = refs[5 + count]
    sums = refs[6 + count : 6 + 2 * count]
    keys_sum, values_sum = refs[6 + 2 * count : 8 + 2 * count]
    scratch = refs[8 + 2 * count :]
    batches, length = seg_row_ref.shape
    width = grad_ref.shape[1]
    shares = (4, 6, 4, 2, 2) if len(bits) == 5 else (1,) * max(1, len(bits))
    stages = shared_out(batches, length, shares)

    def work(stage):
        if stage == 0:
            keys_sum[...] = jnp.zeros_like(keys_sum)
            values_sum[...] = jnp.zeros_like(values_sum)
        for batch, window in stages[stage]:
            attend_rows_back(
                width,
                joined_ref,
                grad_ref,
                norm_ref,
                seg_row_ref,
                seg_col_ref,
                out_ref,
                keys_sum,
                values_sum,
                batch,
                window,
            )
        if stage == len(shares) - 1:
            out_ref[:, width : 2 * width] = (keys_sum[...] * SCORE_SCALE).astype(jnp.bfloat16)
            out_ref[:, 2 * width :] = values_sum[...].astype(jnp.bfloat16)

    if count:
        run_scatter(bits, pieces, parts, sums, scratch, work)
    else:
        for stage in range(len(shares)):
            work(stage)


def attention_back(joined, grad_att, norms, seg_ids, totals, sizes, collective_id):
    batches, length = seg_ids.shape
    rows, width = grad_att.shape
    count = len(totals)
    bits = bits_of(sizes)
    depth = len(bits)
    parts, pieces, scratch = scatter_parts(totals, depth) if count else ([], [], [])
    remote = dict(collective_id=collective_id, has_side_effects=True) if count else {}
    near = pl.BlockSpec(memory_space=pltpu.VMEM)
    out, *sums = pl.pallas_call(
        functools.partial(attention_back_kernel, bits, pieces, count),
        in_specs=[near] * (5 + count),
        out_specs=[near] * (1 + count),
        out_shape=[jax.ShapeDtypeStruct((rows, 3 * width), jnp.bfloat16)]
        + [
            jax.ShapeDtypeStruct((t.shape[0] >> depth, t.shape[1]), jnp.float32) for t in totals
        ],
        scratch_shapes=[pltpu.VMEM((rows, width), jnp.float32)] * 2 + scratch,
        compiler_params=pltpu.CompilerParams(vmem_limit_bytes=56 * MIB, **remote),
        cost_estimate=pl.CostEstimate(
            flops=100 * rows * width * length, bytes_accessed=rows * width * 12, transcendentals=0
        ),
    )(joined, grad_att, norms, seg_ids, seg_ids.reshape(rows, 1), *parts)
    return out, sums


def ffn_kernel(
    second_ref, grad_ref, up_ref, down_ref, bias_ref, out_ref, back_ref, up_sum, down_sum, bias_sum
):
    @pl.when(pl.program_id(0) == 0)
    def _():
        out_ref[...] = jnp.zeros_like(out_ref)
        back_ref[...] = jnp.zeros_like(back_ref)

    second, grad = second_ref[...], grad_ref[...]
    pre = jnp.dot(second, up_ref[...], preferred_element_type=jnp.float32) + bias_ref[...]
    square = pre * pre
    bend = jnp.tanh(GELU_IN * pre * (1.0 + GELU_CUBE * square))
    half = 0.5 + 0.5 * bend
    active = (pre * half).astype(jnp.bfloat16)
    slope = half + 0.5 * pre * (1.0 - bend * bend) * (
        GELU_IN * (1.0 + 3.0 * GELU_CUBE * square)
    )
    out_ref[...] += jnp.dot(active, down_ref[...], preferred_element_type=jnp.float32)
    grad_pre = dot_nt(grad, down_ref[...]) * slope
    low = grad_pre.astype(jnp.bfloat16)
    down_sum[...] = dot_tn(active, grad).astype(down_sum.dtype)
    up_sum[...] = dot_tn(second, low).astype(up_sum.dtype)
    bias_sum[...] = jnp.sum(low.astype(jnp.float32), axis=0, keepdims=True)
    back_ref[...] += dot_nt(low, up_ref[...])


def feed_forward(second, grad_out, w_up, w_down, up_bias):
    rows, width = second.shape
    hidden = w_up.shape[1]
    block = 512 if hidden % 512 == 0 else hidden
    fixed = pl.BlockSpec((rows, width), lambda j: (0, 0))
    across = pl.BlockSpec((width, block), lambda j: (0, j))
    along = pl.BlockSpec((block, width), lambda j: (j, 0))
    line = pl.BlockSpec((1, block), lambda j: (0, j))
    return pl.pallas_call(
        ffn_kernel,
        grid=(hidden // block,),
        in_specs=[fixed, fixed, across, along, line],
        out_specs=[fixed, fixed, across, along, line],
        out_shape=[
            jax.ShapeDtypeStruct((rows, width), jnp.float32),
            jax.ShapeDtypeStruct((rows, width), jnp.float32),
            jax.ShapeDtypeStruct((width, hidden), jnp.bfloat16),
            jax.ShapeDtypeStruct((hidden, width), jnp.bfloat16),
            jax.ShapeDtypeStruct((1, hidden), jnp.float32),
        ],
        compiler_params=pltpu.CompilerParams(vmem_limit_bytes=56 * MIB),
        cost_estimate=pl.CostEstimate(
            flops=12 * rows * width * hidden,
            bytes_accessed=8 * width * hidden + 16 * rows * width,
            transcendentals=rows * hidden,
        ),
    )(second, grad_out, w_up, w_down, up_bias[None])


def norm_rows(inputs, scaling, offset):
    row_mean = jnp.mean(inputs, axis=-1, keepdims=True)
    centred = inputs - row_mean
    spread = jnp.mean(centred * centred, axis=-1, keepdims=True)
    return centred * lax.rsqrt(spread + EPSILON) * scaling + offset


def pack_small(gain, shift, attn, up, down):
    width = -(-max(gain.shape[1], up.shape[0] + down.shape[0]) // 128) * 128
    rows = jnp.concatenate([gain, shift, attn], axis=0).astype(jnp.float32)
    last = jnp.concatenate([up, down]).astype(jnp.float32)
    return jnp.concatenate(
        [
            jnp.pad(rows, ((0, 0), (0, width - rows.shape[1]))),
            jnp.pad(last, (0, width - last.shape[0]))[None],
        ],
        axis=0,
    )


def own_exchange(sizes, shard_rows):
    return powers(sizes) and shard_rows % 8 == 0


def gathered(shard):
    return lax.all_gather(shard, AXES, axis=0, tiled=True)


def scattered(total):
    return lax.psum_scatter(total, AXES, scatter_dimension=0, tiled=True)


def local(
    sizes,
    tokens,
    seg_ids,
    w_qkv,
    w_out,
    w_up,
    w_down,
    ln_gain,
    ln_bias,
    bias_attn,
    bias_up,
    bias_down,
    grad_out,
):
    devices = sizes[0] * sizes[1]
    model_width = tokens.shape[1]
    own = ln_gain.shape[1]
    own_up = bias_up.shape[0]
    direct = own_exchange(sizes, w_qkv.shape[0])
    small = pack_small(ln_gain, ln_bias, bias_attn, bias_up, bias_down)
    small_shape = small.shape
    if direct:
        w_qkv, small = gather_all([w_qkv, small], sizes, 1)
        w_qkv, small, w_down = lax.optimization_barrier((w_qkv, small, w_down))
    else:
        w_qkv, small, w_out, w_up = (gathered(t) for t in (w_qkv, small, w_out, w_up))
    w_down = gathered(w_down)
    small = small.reshape((devices,) + small_shape)
    features = jnp.swapaxes(small[:, :7, :own], 0, 1).reshape(7, devices * own)
    gains, shifts, attn_bias = features[0:2], features[2:4], features[4:7]
    up_bias = small[:, 7, :own_up].reshape(-1)
    down_bias = small[:, 7, own_up : own_up + own].reshape(-1)

    rows_float = tokens.astype(jnp.float32)
    normed, norm_one = jax.vjp(norm_rows, rows_float, gains[0], shifts[0])
    normed_low = normed.astype(jnp.bfloat16)
    zero_bias = jnp.zeros((model_width,), jnp.float32)
    qkv_bias = jnp.concatenate([attn_bias[0], zero_bias, attn_bias[1]])
    joined = (jnp.dot(normed_low, w_qkv, preferred_element_type=jnp.float32) + qkv_bias).astype(
        jnp.bfloat16
    )
    attended, norms, moved = attention(
        joined, seg_ids, [w_out, w_up] if direct else [], sizes, 2
    )
    if direct:
        w_out, w_up = moved
    residual = (
        rows_float + jnp.dot(attended, w_out, preferred_element_type=jnp.float32) + attn_bias[2]
    )
    second, norm_two = jax.vjp(norm_rows, residual, gains[1], shifts[1])
    second_low = second.astype(jnp.bfloat16)
    ffn_out, grad_second, up_sum, down_sum, upb_sum = feed_forward(
        second_low, grad_out, w_up, w_down, up_bias
    )
    layer_out = (residual + ffn_out + down_bias).astype(jnp.bfloat16)
    down_sum = scattered(down_sum).astype(jnp.float32)

    grad_float = grad_out.astype(jnp.float32)
    downb_sum = jnp.sum(grad_float, axis=0)
    grad_resid, gain_two, shift_two = norm_two(grad_second)
    grad_resid = grad_resid + grad_float
    grad_resid_low = grad_resid.astype(jnp.bfloat16)
    out_sum = dot_tn(attended, grad_resid_low).astype(jnp.bfloat16)
    bias_out_grad = jnp.sum(grad_resid_low.astype(jnp.float32), axis=0)
    grad_att = dot_nt(grad_resid_low, w_out).astype(jnp.bfloat16)
    grad_joined, moved = attention_back(
        joined, grad_att, norms, seg_ids, [up_sum, out_sum] if direct else [], sizes, 3
    )
    if direct:
        up_sum, out_sum = moved
    qkv_sum = dot_tn(normed_low, grad_joined).astype(jnp.bfloat16)
    joined_bias = jnp.sum(grad_joined.astype(jnp.float32), axis=0)
    grad_normed = dot_nt(grad_joined, w_qkv)
    grad_input, gain_one, shift_one = norm_one(grad_normed)
    grad_tokens = (grad_resid + grad_input).astype(jnp.bfloat16)

    features = jnp.stack(
        [
            gain_one,
            gain_two,
            shift_one,
            shift_two,
            joined_bias[:model_width],
            joined_bias[2 * model_width :],
            bias_out_grad,
        ]
    )
    features = jnp.swapaxes(features.reshape(7, devices, own), 0, 1)
    last = jnp.concatenate(
        [upb_sum.reshape(devices, own_up), downb_sum.reshape(devices, own)], axis=1
    )
    width = small.shape[2]
    packed = jnp.concatenate(
        [
            jnp.pad(features, ((0, 0), (0, 0), (0, width - own))),
            jnp.pad(last, ((0, 0), (0, width - last.shape[1])))[:, None],
        ],
        axis=1,
    )
    packed = packed.reshape(-1, width)
    if direct:
        qkv_sum, packed = scatter_all([qkv_sum, packed], sizes, 4)
    else:
        qkv_sum, out_sum, up_sum, packed = (
            scattered(t.astype(jnp.float32)) for t in (qkv_sum, out_sum, up_sum, packed)
        )
    return (
        layer_out,
        grad_tokens,
        qkv_sum,
        out_sum,
        up_sum,
        down_sum,
        packed[0:2, :own],
        packed[2:4, :own],
        packed[4:7, :own],
        packed[7, :own_up],
        packed[7, own_up : own_up + own],
    )


def solution(mesh):
    return jax.shard_map(
        functools.partial(local, (mesh.shape["fsdp"], mesh.shape["rep"])),
        mesh=mesh,
        in_specs=(
            P(("fsdp", "rep"), None),
            P(("fsdp", "rep"), None),
            P(("fsdp", "rep"), None),
            P(("fsdp", "rep"), None),
            P(("fsdp", "rep"), None),
            P(("fsdp", "rep"), None),
            P(None, ("fsdp", "rep")),
            P(None, ("fsdp", "rep")),
            P(None, ("fsdp", "rep")),
            P(("fsdp", "rep")),
            P(("fsdp", "rep")),
            P(("fsdp", "rep"), None),
        ),
        out_specs=(
            P(("fsdp", "rep"), None),
            P(("fsdp", "rep"), None),
            P(("fsdp", "rep"), None),
            P(("fsdp", "rep"), None),
            P(("fsdp", "rep"), None),
            P(("fsdp", "rep"), None),
            P(None, ("fsdp", "rep")),
            P(None, ("fsdp", "rep")),
            P(None, ("fsdp", "rep")),
            P(("fsdp", "rep")),
            P(("fsdp", "rep")),
        ),
        check_vma=False,
    )
```
